32 devices in a mesh: groups: 2 (over x), gx: 8 (over z, y), gy: 2 (over core).
Axes of the slice: x: 2, y: 2, z: 4, core: 2. Of those that a mesh axis runs over, the one named last changes fastest.
Arguments:
- field: float32 [128, 128, 1024], P(('groups', 'gx'), 'gy'), parts along dimension 0, may hold values from -6 to 6
- spectral: float32 [2, 32, 2, 32, 8192], P(None, 'gx', None, 'gy'), may hold values from -6 to 6
- mixing: float32 [2, 16, 16], replicated, may hold values from -1.5 to 1.5
- bias: float32 [2, 16], replicated, may hold values from -3 to 3
Outputs:
- result: float32 [128, 128, 1024], P(('groups', 'gx'), 'gy'), parts along dimension 0
The draws below stay inside these ranges and needn't reach their ends.
There are 2 independent parts, one for each index of `groups`. The reference program is written for one: setup_inputs(seed, part) draws one part's arguments, and reference() takes and returns one part's arrays. A program takes and returns all parts, laid end to end along the dimension named above; an argument that names none is the same for every part. Nothing has to cross between parts.
All inputs are finite; a program needn't handle non-finite values.
Results may differ from the reference program's by a relative error of at most 0.0001.
Values sent between devices are 32-bit elements; how exact they have to be, the bound alone decides.
A program may use at most 192 MiB of HBM per device.

```python
import math
import jax
import jax.numpy as jnp
from jax import lax

C = 16
MX = 32
MY = 32
MZ = 32
NZ = 64
LAYERS = 2
NX = 64
NY = 128


def shard_levels(key, extent, cuts, least, largest):
    loudness = 1.0
    for axis_at, blocks in cuts:
        draws = jax.random.uniform(jax.random.fold_in(jax.random.fold_in(key, 6), axis_at), (blocks,), jnp.float32, least / len(cuts), largest / len(cuts))
        loudness = loudness * jnp.repeat(jnp.exp(draws), extent[axis_at] // blocks).reshape((-1,) + (1,) * (len(extent) - 1 - axis_at))
    return loudness


def scatter_about(rng, extent, deviation, bound, cuts=(), held_as=jnp.bfloat16):
    entries = jax.random.normal(rng, extent, jnp.float32) * deviation
    if len(cuts) > 0:
        entries = shard_levels(rng, extent, cuts, -0.22, 0.18) * entries
    return jnp.clip(entries, min=-bound, max=bound).astype(held_as)


def setup_inputs(seed: int = 0, part: int = 0) -> dict:
    key_of = jax.random.split(jax.random.key(seed), 5)
    own_keys = jax.random.split(jax.random.fold_in(key_of[4], part), 5)
    return {
        "field": scatter_about(own_keys[0], (NX, NY, NZ * C), 1.0, 6.0, ((0, 8), (1, 2)), jnp.float32),
        "spectral": scatter_about(key_of[1], (LAYERS, MX, 2, MY, MZ * C * C), 1.0, 6.0, ((1, 8), (3, 2)), jnp.float32),
        "mixing": scatter_about(key_of[2], (LAYERS, C, C), C ** -0.5, 1.5, (), jnp.float32),
        "bias": scatter_about(key_of[3], (LAYERS, C), 0.5, 3.0, (), jnp.float32),
    }


def contract(form, left, right):
    return jnp.einsum(form, left, right, precision=lax.Precision.HIGHEST)


def signed_modes(count):
    half = count // 2
    return jnp.concatenate([jnp.arange(half, dtype=jnp.int32), jnp.arange(half, dtype=jnp.int32) - half]).astype(jnp.int32)


def phase(frequencies, positions, length):
    turns = jnp.mod(frequencies[:, None] * positions[None, :], length).astype(jnp.float32)
    angle = turns * (2.0 * math.pi / length)
    return jnp.cos(angle), jnp.sin(angle)


def reference(field, spectral, mixing, bias):
    signal = field.reshape(NX, NY, NZ, C)
    x_modes = signed_modes(MX)
    y_modes = signed_modes(MY)
    z_cosine, z_sine = phase(jnp.arange(MZ, dtype=jnp.int32), jnp.arange(NZ, dtype=jnp.int32), NZ)
    z_weights = jnp.where(jnp.arange(MZ) == 0, 1.0, 2.0).astype(jnp.float32) / (NX * NY * NZ)
    back_cosine = z_cosine * z_weights[:, None]
    back_sine = z_sine * z_weights[:, None]
    y_cosine, y_sine = phase(y_modes, jnp.arange(NY, dtype=jnp.int32), NY)
    x_cosine, x_sine = phase(x_modes, jnp.arange(NX, dtype=jnp.int32), NX)
    for layer in range(LAYERS):
        z_real = contract('xyzc,kz->xykc', signal, z_cosine)
        z_imaginary = -contract('xyzc,kz->xykc', signal, z_sine)
        y_real = contract('xykc,qy->xqkc', z_real, y_cosine) + contract('xykc,qy->xqkc', z_imaginary, y_sine)
        y_imaginary = contract('xykc,qy->xqkc', z_imaginary, y_cosine) - contract('xykc,qy->xqkc', z_real, y_sine)
        x_real = contract('xqkc,px->pqkc', y_real, x_cosine) + contract('xqkc,px->pqkc', y_imaginary, x_sine)
        x_imaginary = contract('xqkc,px->pqkc', y_imaginary, x_cosine) - contract('xqkc,px->pqkc', y_real, x_sine)
        tensor = spectral[layer].reshape(MX, 2, MY, MZ, C, C)
        mixed_real = contract('pqkc,pqkco->pqko', x_real, tensor[:, 0]) - contract('pqkc,pqkco->pqko', x_imaginary, tensor[:, 1])
        mixed_imaginary = contract('pqkc,pqkco->pqko', x_real, tensor[:, 1]) + contract('pqkc,pqkco->pqko', x_imaginary, tensor[:, 0])
        back_x_real = contract('pqko,px->xqko', mixed_real, x_cosine) - contract('pqko,px->xqko', mixed_imaginary, x_sine)
        back_x_imaginary = contract('pqko,px->xqko', mixed_imaginary, x_cosine) + contract('pqko,px->xqko', mixed_real, x_sine)
        back_y_real = contract('xqko,qy->xyko', back_x_real, y_cosine) - contract('xqko,qy->xyko', back_x_imaginary, y_sine)
        back_y_imaginary = contract('xqko,qy->xyko', back_x_imaginary, y_cosine) + contract('xqko,qy->xyko', back_x_real, y_sine)
        spatial = contract('xyko,kz->xyzo', back_y_real, back_cosine) - contract('xyko,kz->xyzo', back_y_imaginary, back_sine)
        local = contract('xyzc,co->xyzo', signal, mixing[layer]) + bias[layer]
        signal = jax.nn.gelu(spatial + local, approximate=False)
    return signal.reshape(NX, NY, NZ * C)
```

```python
import functools
import math

import jax
import jax.numpy as jnp
import ml_dtypes
import numpy as np
from jax import lax
from jax.experimental import pallas as pl
from jax.experimental.pallas import tpu as pltpu
from jax.sharding import PartitionSpec as P

C = 16
MX = 32
MY = 32
MZ = 32
NZ = 64
LAYERS = 2
WIDTH = MZ * C
LANES = NZ * C
CHUNKS = 2
CW = WIDTH // CHUNKS
BLOCKS = CW // 128
MESH = pl.DeviceIdType.MESH


def signed_modes(count):
    half = count // 2
    return np.concatenate([np.arange(half), np.arange(half) - half])


def waves(frequencies, positions, length):
    angle = 2.0 * math.pi * ((frequencies[:, None] * positions[None, :]) % length) / length
    return np.cos(angle), np.sin(angle)


def pair(matrix):
    high = matrix.astype(np.float32).astype(ml_dtypes.bfloat16)
    low = (matrix - high.astype(np.float64)).astype(np.float32).astype(ml_dtypes.bfloat16)
    return np.stack([high, low])


def complex_rows(cosine, sine, sign):
    return np.stack([np.stack([cosine, -sign * sine], -1), np.stack([sign * sine, cosine], -1)], -2)


@functools.lru_cache(None)
def tables(n, pair_size, cells_x, cells_y):
    span_x, span_y = cells_x * n, cells_y * pair_size
    qs = MY // pair_size
    qn, pn = qs // n, MX // n
    eye = np.eye
    cosine, sine = waves(np.arange(MZ), np.arange(NZ), NZ)
    channels = eye(C)
    z_forward = np.einsum("pkz,cd->zcpkd", np.stack([cosine, -sine]), channels).reshape(LANES, 2 * WIDTH)
    scale = np.where(np.arange(MZ) == 0, 1.0, 2.0)[:, None] / (span_x * span_y * NZ)
    z_backward = np.einsum("pkz,cd->pkczd", np.stack([cosine * scale, -sine * scale]), channels).reshape(
        2 * WIDTH, LANES
    )
    y_forward, y_backward = [], []
    for g in range(pair_size):
        cosine, sine = waves(signed_modes(MY), g * cells_y + np.arange(cells_y), span_y)
        forward = complex_rows(cosine, sine, -1).reshape(pair_size, n, qn, cells_y, 2, 2)
        y_forward.append(
            pair(
                np.einsum("hdqyab,xw->hdxqabwy", forward, eye(cells_x)).reshape(
                    pair_size * n * cells_x * qn * 2, 2 * cells_x * cells_y
                )
            )
        )
        backward = complex_rows(cosine, sine, 1).reshape(pair_size, n, qn, cells_y, 2, 2)
        y_backward.append(
            pair(
                np.einsum("hdqyab,xw->awyhdxqb", backward, eye(cells_x)).reshape(
                    2 * cells_x * cells_y, pair_size * n * cells_x * qn * 2
                )
            )
        )
    cosine, sine = waves(signed_modes(MX), np.arange(span_x), span_x)
    rows = pn * qn * 2
    padded = max(8, rows)
    forward = complex_rows(cosine, sine, -1).reshape(n, pn, n, cells_x, 2, 2)
    x_forward = np.einsum("dpsxab,qr->dpqasxrb", forward, eye(qn)).reshape(n, rows, -1)
    x_forward = np.pad(x_forward, ((0, 0), (0, padded - rows), (0, 0))).reshape(n * padded, -1)
    backward = complex_rows(cosine, sine, 1).reshape(n, pn, n, cells_x, 2, 2)
    x_backward = np.einsum("dpsxab,qr->sxqadprb", backward, eye(qn)).reshape(-1, n, rows)
    x_backward = np.pad(x_backward, ((0, 0), (0, 0), (0, padded - rows))).reshape(-1, n * padded)
    order = np.zeros((pn, 2, n, qn, n, padded))
    for p in range(pn):
        for part in range(2):
            for s in range(n):
                for q in range(qn):
                    order[p, part, s, q, s, (p * qn + q) * 2 + part] = 1.0
    order = order.reshape(pn * 2 * qs, n * padded)
    spread = np.einsum("kl,cd,o->lckdo", eye(8), channels, np.ones(C)).reshape(128, 8, C * C)
    spread = np.concatenate([spread, spread]).transpose(1, 0, 2)
    gather = np.einsum("kl,c,op->kcolp", eye(8), np.ones(C), channels).reshape(8, C * C, 128)
    cast = lambda a: np.ascontiguousarray(a).astype(ml_dtypes.bfloat16)
    return dict(
        zf=pair(z_forward),
        zb=pair(z_backward),
        yf=np.stack(y_forward),
        yb=np.stack(y_backward),
        xf=pair(x_forward),
        xb=pair(x_backward),
        order=cast(order),
        back=cast(order.T),
        spread=cast(spread),
        gather=cast(gather),
    )


def split(value):
    high = value.astype(jnp.bfloat16)
    return high, (value - high.astype(jnp.float32)).astype(jnp.bfloat16)


def dot(left, right):
    return jnp.dot(left, right, preferred_element_type=jnp.float32)


def dot3(left, right):
    return dot(left[0], right[0]) + (dot(left[0], right[1]) + dot(left[1], right[0]))


def erf(x):
    x = jnp.clip(x, -4.0, 4.0)
    square = x * x
    top = jnp.float32(-2.72614225801306e-10)
    for c in (2.77068142495902e-08, -2.10102402082508e-06, -5.69250639462346e-05,
              -7.34990630326855e-04, -2.95459980854025e-03, -1.60960333262415e-02):
        top = top * square + c
    bottom = jnp.float32(-1.45660718464996e-05)
    for c in (-2.13374055278905e-04, -1.68282697438203e-03, -7.37332916720468e-03, -1.42647390514189e-02):
        bottom = bottom * square + c
    return x * top / bottom


def kernel(n, pn, cells, *refs):
    names = ("field", "spectral", "local", "bias", "zf", "yf", "xf", "order", "spread", "gather",
             "back", "xb", "yb", "zb")
    hbm = dict(zip(names, refs))
    out_hbm = refs[len(names)]
    (signal, weights, local, bias, zf, yf, xf, order, spread, gather, back, xb, yb, zb,
     s_high, s_low, z_high, z_low, b_high, b_low, p_high, p_low, total,
     send_y, recv_y, send_1, recv_1, send_2, recv_2, send_3, recv_3, send_4, recv_4, both,
     load_sem, pair_send, pair_recv, ring_send, ring_recv) = refs[len(names) + 1:]
    me = lax.axis_index("gx")
    core = lax.axis_index("gy")
    other = 1 - core
    rows_x = recv_1.shape[3]
    half = n * rows_x
    here = dict(field=signal, spectral=weights, local=local, bias=bias, zf=zf, yf=yf, xf=xf, order=order,
                spread=spread, gather=gather, back=back, xb=xb, yb=yb, zb=zb)
    loads = {}
    for at, name in enumerate(("field", "zf", "yf", "xf", "order", "spread", "spectral", "gather", "back", "xb",
                               "yb", "local", "bias", "zb")):
        source = hbm[name].at[core] if name in ("yf", "yb") else hbm[name]
        loads[name] = pltpu.make_async_copy(source, here[name], load_sem.at[at])
        loads[name].start()

    barrier = pltpu.get_barrier_semaphore()

    def greet(k, _):
        pl.semaphore_signal(barrier, inc=1, device_id={"gx": lax.rem(me + k, n)}, device_id_type=MESH)
        return 0

    lax.fori_loop(1, n, greet, 0)
    pl.semaphore_signal(barrier, inc=1, device_id={"gy": other}, device_id_type=MESH)
    pl.semaphore_wait(barrier, n)

    loads["field"].wait()

    def split_rows(i, _):
        at = pl.ds(pl.multiple_of(i * 64, 64), 64)
        s_high[at, :], s_low[at, :] = split(signal[at, :])
        return 0

    lax.fori_loop(0, cells // 64, split_rows, 0)
    for name in ("zf", "yf", "xf", "order", "spread", "spectral", "gather", "back", "xb", "yb", "local", "bias", "zb"):
        loads[name].wait()

    def ring_copy(stage, send, recv, layer, j, peer, slot, index):
        return pltpu.make_async_remote_copy(
            src_ref=send.at[layer, j, peer],
            dst_ref=recv.at[layer, j, slot],
            send_sem=ring_send.at[stage, layer, j, peer],
            recv_sem=ring_recv.at[stage, layer, j, slot],
            device_id={"gx": index},
            device_id_type=MESH,
        )

    def exchange(stage, send, recv, layer, j):
        def start(k, _):
            peer = lax.rem(me + k, n)
            ring_copy(stage, send, recv, layer, j, peer, me, peer).start()
            return 0

        lax.fori_loop(1, n, start, 0)
        recv[layer, j, me] = send[layer, j, me]

    def arrive(stage, send, recv, layer, j):
        def wait(k, _):
            peer = lax.rem(me + k, n)
            ring_copy(stage, send, recv, layer, j, peer, peer, peer).wait()
            return 0

        lax.fori_loop(1, n, wait, 0)

    def pair_copy(stage, send, recv, layer, j):
        return pltpu.make_async_remote_copy(
            src_ref=send,
            dst_ref=recv,
            send_sem=pair_send.at[stage, layer, j],
            recv_sem=pair_recv.at[stage, layer, j],
            device_id={"gy": other},
            device_id_type=MESH,
        )

    def run_layer(layer, _):
        def z_forward(t, _):
            lanes = pl.ds(pl.multiple_of(t * 256, 256), 256)
            value = dot3((s_high[...], s_low[...]), (zf[0, :, lanes], zf[1, :, lanes]))
            per = WIDTH // 256
            rows = pl.ds(pl.multiple_of((t // per) * cells, cells), cells)
            to = pl.ds(pl.multiple_of((t % per) * 256, 256), 256)
            z_high[rows, to], z_low[rows, to] = split(value)
            return 0

        def y_part(which, j):
            lanes = pl.ds(pl.multiple_of(j * CW, CW), CW)
            rows = pl.ds(pl.multiple_of(which * half, half), half)
            return dot3((yf[0, rows, :], yf[1, rows, :]), (z_high[:, lanes], z_low[:, lanes]))

        def y_forward(j, _):
            z_forward(j, 0)
            z_forward(j + CHUNKS, 0)
            send_y[layer, j] = y_part(other, j)
            pair_copy(0, send_y.at[layer, j], recv_y.at[layer, j], layer, j).start()
            send_1[layer, j] = y_part(core, j).reshape(n, rows_x, CW)
            return 0

        lax.fori_loop(0, CHUNKS, y_forward, 0)

        def x_send(j, _):
            pair_copy(0, send_y.at[layer, j], recv_y.at[layer, j], layer, j).wait()
            send_1[layer, j] = send_1[layer, j] + recv_y[layer, j].reshape(n, rows_x, CW)
            exchange(0, send_1, recv_1, layer, j)
            return 0

        lax.fori_loop(0, CHUNKS, x_send, 0)

        def x_forward(j, _):
            arrive(0, send_1, recv_1, layer, j)
            value = dot3((xf[0], xf[1]), split(recv_1[layer, j].reshape(half, CW)))
            send_2[layer, j] = value.reshape(send_2.shape[2:])
            exchange(1, send_2, recv_2, layer, j)
            return 0

        lax.fori_loop(0, CHUNKS, x_forward, 0)

        def mix(j, _):
            arrive(1, send_2, recv_2, layer, j)
            high, low = split(recv_2[layer, j].reshape(order.shape[1], CW))
            high = dot(order[...], high).astype(jnp.bfloat16)
            low = dot(order[...], low).astype(jnp.bfloat16)
            kept = order.shape[0]
            left = jnp.concatenate(
                [
                    jnp.concatenate([high[:, b * 128:(b + 1) * 128], low[:, b * 128:(b + 1) * 128]], 1)
                    for b in range(BLOCKS)
                ],
                0,
            )
            total[...] = jnp.zeros_like(total)

            def one_mode(k, _):
                modes = dot(left, spread[k])
                for b in range(BLOCKS):
                    lanes = pl.ds(pl.multiple_of(((j * BLOCKS + b) * 8 + k) * 256, 256), 256)
                    for p in range(pn):
                        at = b * kept + p * 32
                        real, imaginary = modes[at:at + 16], modes[at + 16:at + 32]
                        w_real = weights[layer, p, 0, :, lanes]
                        w_imaginary = weights[layer, p, 1, :, lanes]
                        p_high[at:at + 16, :], p_low[at:at + 16, :] = split(real * w_real - imaginary * w_imaginary)
                        p_high[at + 16:at + 32, :], p_low[at + 16:at + 32, :] = split(
                            real * w_imaginary + imaginary * w_real
                        )
                total[...] += dot(p_high[...], gather[k]) + dot(p_low[...], gather[k])
                return 0

            lax.fori_loop(0, 8, one_mode, 0)
            mixed = jnp.concatenate([total[b * kept:(b + 1) * kept, :] for b in range(BLOCKS)], 1)
            high, low = split(mixed)
            send_3[layer, j] = (dot(back[...], high) + dot(back[...], low)).reshape(send_3.shape[2:])
            exchange(2, send_3, recv_3, layer, j)
            return 0

        lax.fori_loop(0, CHUNKS, mix, 0)

        def x_backward(j, _):
            arrive(2, send_3, recv_3, layer, j)
            value = dot3((xb[0], xb[1]), split(recv_3[layer, j].reshape(order.shape[1], CW)))
            send_4[layer, j] = value.reshape(n, rows_x, CW)
            exchange(3, send_4, recv_4, layer, j)
            return 0

        lax.fori_loop(0, CHUNKS, x_backward, 0)

        def y_send(j, _):
            arrive(3, send_4, recv_4, layer, j)
            both[layer, j, core] = recv_4[layer, j].reshape(half, CW)
            pair_copy(1, both.at[layer, j, core], both.at[layer, j, core], layer, j).start()
            return 0

        lax.fori_loop(0, CHUNKS, y_send, 0)

        def y_backward(j, _):
            pair_copy(1, both.at[layer, j, core], both.at[layer, j, other], layer, j).wait()
            high, low = split(both[layer, j].reshape(2 * half, CW))
            for part in range(2):
                at = slice(part * cells, (part + 1) * cells)
                value = dot3((yb[0, at, :], yb[1, at, :]), (high, low))
                lanes = pl.ds(pl.multiple_of(part * WIDTH + j * CW, CW), CW)
                b_high[:, lanes], b_low[:, lanes] = split(value)
            return 0

        lax.fori_loop(0, CHUNKS, y_backward, 0)
        local_pair = split(local[layer])

        def z_backward(t, _):
            lanes = pl.ds(pl.multiple_of(t * 256, 256), 256)
            value = dot3((b_high[...], b_low[...]), (zb[0, :, lanes], zb[1, :, lanes]))
            value += dot3((s_high[:, lanes], s_low[:, lanes]), local_pair)
            value += bias[layer]
            value = 0.5 * value * (1.0 + erf(value * math.sqrt(0.5)))
            signal[:, lanes] = value
            s_high[:, lanes], s_low[:, lanes] = split(value)
            return 0

        lax.fori_loop(0, LANES // 256, z_backward, 0)
        return 0

    lax.fori_loop(0, LAYERS, run_layer, 0)
    store = pltpu.make_async_copy(signal, out_hbm, load_sem.at[0])
    store.start()
    store.wait()


def shards(field, spectral, mixing, bias):
    cells_x, cells_y = field.shape[:2]
    n, pair_size = lax.axis_size("gx"), lax.axis_size("gy")
    cells = cells_x * cells_y
    table = tables(n, pair_size, cells_x, cells_y)
    pn = spectral.shape[1]
    qs = spectral.shape[3]
    rows_x = cells_x * (qs // n) * 2
    rows_p = table["xf"].shape[1] // n
    local = jnp.tile(mixing, (1, 16, 16)) * jnp.asarray(np.kron(np.eye(16), np.ones((C, C))), jnp.float32)
    wide_bias = jnp.tile(bias, (1, 16))[:, None, :]
    operands = [field.reshape(cells, LANES), spectral, local, wide_bias] + [
        jnp.asarray(table[name])
        for name in ("zf", "yf", "xf", "order", "spread", "gather", "back", "xb", "yb", "zb")
    ]
    f32, bf16 = jnp.float32, jnp.bfloat16
    loaded = []
    for at, operand in enumerate(operands):
        shape = operand.shape[1:] if at in (5, 12) else operand.shape
        loaded.append(pltpu.VMEM(shape, operand.dtype))
    half = n * rows_x
    kept = pn * 2 * qs
    scratch = loaded + [
        pltpu.VMEM((cells, LANES), bf16),
        pltpu.VMEM((cells, LANES), bf16),
        pltpu.VMEM((2 * cells, WIDTH), bf16),
        pltpu.VMEM((2 * cells, WIDTH), bf16),
        pltpu.VMEM((cells, 2 * WIDTH), bf16),
        pltpu.VMEM((cells, 2 * WIDTH), bf16),
        pltpu.VMEM((BLOCKS * kept, 256), bf16),
        pltpu.VMEM((BLOCKS * kept, 256), bf16),
        pltpu.VMEM((BLOCKS * kept, 128), f32),
        pltpu.VMEM((LAYERS, CHUNKS, half, CW), f32),
        pltpu.VMEM((LAYERS, CHUNKS, half, CW), f32),
    ]
    for rows in (rows_x, rows_p, rows_p, rows_x):
        scratch += [pltpu.VMEM((LAYERS, CHUNKS, n, rows, CW), f32)] * 2
    scratch += [
        pltpu.VMEM((LAYERS, CHUNKS, 2, half, CW), f32),
        pltpu.SemaphoreType.DMA((len(operands),)),
        pltpu.SemaphoreType.DMA((2, LAYERS, CHUNKS)),
        pltpu.SemaphoreType.DMA((2, LAYERS, CHUNKS)),
        pltpu.SemaphoreType.DMA((4, LAYERS, CHUNKS, n)),
        pltpu.SemaphoreType.DMA((4, LAYERS, CHUNKS, n)),
    ]
    result = pl.pallas_call(
        functools.partial(kernel, n, pn, cells),
        out_shape=jax.ShapeDtypeStruct((cells, LANES), f32),
        in_specs=[pl.BlockSpec(memory_space=pl.ANY)] * len(operands),
        out_specs=pl.BlockSpec(memory_space=pl.ANY),
        scratch_shapes=scratch,
        compiler_params=pltpu.CompilerParams(
            collective_id=0, has_side_effects=True, vmem_limit_bytes=60 * 1024 * 1024
        ),
    )(*operands)
    return result.reshape(cells_x, cells_y, LANES)


def solution(mesh):
    placed = (P(("groups", "gx"), "gy", None), P(None, "gx", None, "gy", None), P(), P())
    return jax.shard_map(
        shards,
        mesh=mesh,
        in_specs=placed,
        out_specs=P(("groups", "gx"), "gy", None),
        check_vma=False,
    )
```

```python
import functools
import math

import jax
import jax.numpy as jnp
import ml_dtypes
import numpy as np
from jax import lax
from jax.experimental import pallas as pl
from jax.experimental.pallas import tpu as pltpu
from jax.sharding import PartitionSpec as P

C = 16
MX = 32
MY = 32
MZ = 32
NZ = 64
LAYERS = 2
WIDTH = MZ * C
LANES = NZ * C
CHUNKS = 2
CW = WIDTH // CHUNKS
BLOCKS = CW // 128
UNROLL = 4
HALVES = 2
MESH = pl.DeviceIdType.MESH


def signed_modes(count):
    half = count // 2
    return np.concatenate([np.arange(half), np.arange(half) - half])


def waves(frequencies, positions, length):
    angle = 2.0 * math.pi * ((frequencies[:, None] * positions[None, :]) % length) / length
    return np.cos(angle), np.sin(angle)


def pair(matrix):
    high = matrix.astype(np.float32).astype(ml_dtypes.bfloat16)
    low = (matrix - high.astype(np.float64)).astype(np.float32).astype(ml_dtypes.bfloat16)
    return np.stack([high, low])


def complex_rows(cosine, sine, sign):
    return np.stack([np.stack([cosine, -sign * sine], -1), np.stack([sign * sine, cosine], -1)], -2)


@functools.lru_cache(None)
def tables(n, pair_size, cells_x, cells_y):
    span_x, span_y = cells_x * n, cells_y * pair_size
    qs = MY // pair_size
    qn, pn = qs // n, MX // n
    eye = np.eye
    part_x = cells_x // HALVES
    cosine, sine = waves(np.arange(MZ), np.arange(NZ), NZ)
    channels = eye(C)
    z_forward = np.einsum("pkz,cd->zcpkd", np.stack([cosine, -sine]), channels).reshape(LANES, 2 * WIDTH)
    scale = np.where(np.arange(MZ) == 0, 1.0, 2.0)[:, None] / (span_x * span_y * NZ)
    z_backward = np.einsum("pkz,cd->pkczd", np.stack([cosine * scale, -sine * scale]), channels).reshape(
        2 * WIDTH, LANES
    )
    y_forward, y_backward = [], []
    for g in range(pair_size):
        cosine, sine = waves(signed_modes(MY), g * cells_y + np.arange(cells_y), span_y)
        forward = complex_rows(cosine, sine, -1).reshape(pair_size, n, qn, cells_y, 2, 2)
        y_forward.append(
            pair(
                np.einsum("hdqyab,xw->hdxqabwy", forward, eye(part_x)).reshape(
                    pair_size * n * part_x * qn * 2, 2 * part_x * cells_y
                )
            )
        )
        backward = complex_rows(cosine, sine, 1).reshape(pair_size, n, qn, cells_y, 2, 2)
        y_backward.append(
            pair(
                np.einsum("hdqyab,xw->awyhdxqb", backward, eye(part_x)).reshape(
                    2 * part_x * cells_y, pair_size * n * part_x * qn * 2
                )
            )
        )
    cosine, sine = waves(signed_modes(MX), np.arange(span_x), span_x)
    rows = pn * qn * 2
    padded = max(8, rows)
    forward = complex_rows(cosine, sine, -1).reshape(n, pn, n, HALVES, part_x, 2, 2)
    x_forward = np.einsum("dpshxab,qr->dpqahsxrb", forward, eye(qn)).reshape(n, rows, -1)
    x_forward = np.pad(x_forward, ((0, 0), (0, padded - rows), (0, 0))).reshape(n * padded, -1)
    backward = complex_rows(cosine, sine, 1).reshape(n, pn, n, HALVES, part_x, 2, 2)
    x_backward = np.einsum("dpshxab,qr->hsxqadprb", backward, eye(qn)).reshape(-1, n, rows)
    x_backward = np.pad(x_backward, ((0, 0), (0, 0), (0, padded - rows))).reshape(-1, n * padded)
    order = np.zeros((pn, 2, n, qn, n, padded))
    for p in range(pn):
        for part in range(2):
            for s in range(n):
                for q in range(qn):
                    order[p, part, s, q, s, (p * qn + q) * 2 + part] = 1.0
    order = order.reshape(pn * 2 * qs, n * padded)
    spread = np.einsum("kl,cd,o->lckdo", eye(8), channels, np.ones(C)).reshape(128, 8, C * C)
    spread = np.concatenate([spread, spread]).transpose(1, 0, 2)
    gather = np.einsum("kl,c,op->kcolp", eye(8), np.ones(8), channels).reshape(8, 128, 128)
    gather = np.concatenate([gather, gather], 1).reshape(8 * 256, 128)
    tile = np.kron(np.ones((16, 1)), channels)
    cast = lambda a: np.ascontiguousarray(a).astype(ml_dtypes.bfloat16)
    return dict(
        zf=pair(z_forward),
        zb=pair(z_backward),
        yf=np.stack(y_forward),
        yb=np.stack(y_backward),
        xf=pair(x_forward),
        xb=pair(x_backward),
        order=cast(order),
        back=cast(order.T),
        spread=cast(spread),
        gather=cast(gather),
        tile=cast(tile),
        across=cast(tile.T),
    )


def split(value):
    high = value.astype(jnp.bfloat16)
    return high, (value - high.astype(jnp.float32)).astype(jnp.bfloat16)


def dot(left, right):
    return jnp.dot(left, right, preferred_element_type=jnp.float32)


def dot3(left, right):
    return dot(left[0], right[0]) + (dot(left[0], right[1]) + dot(left[1], right[0]))


def erf(x):
    x = jnp.clip(x, -4.0, 4.0)
    square = x * x
    top = jnp.float32(-2.72614225801306e-10)
    for c in (2.77068142495902e-08, -2.10102402082508e-06, -5.69250639462346e-05,
              -7.34990630326855e-04, -2.95459980854025e-03, -1.60960333262415e-02):
        top = top * square + c
    bottom = jnp.float32(-1.45660718464996e-05)
    for c in (-2.13374055278905e-04, -1.68282697438203e-03, -7.37332916720468e-03, -1.42647390514189e-02):
        bottom = bottom * square + c
    return x * top / bottom


def kernel(n, pn, cells, *refs):
    names = ("field", "spectral", "mixing", "bias", "zf", "yf", "xf", "order", "spread", "gather",
             "back", "xb", "yb", "zb", "tile", "across")
    hbm = dict(zip(names, refs))
    out_hbm = refs[len(names)]
    (signal, weights, mixing, bias, zf, yf, xf, order, spread, gather, back, xb, yb, zb, tile, across,
     s_high, s_low, z_high, z_low, b_high, b_low, product, local_high, local_low, wide_bias,
     send_y, recv_y, send_1, recv_1, send_2, recv_2, send_3, recv_3, send_4, recv_4, both,
     load_sem, store_sem, pair_send, pair_recv, outer_send, outer_recv, inner_send, inner_recv) = refs[len(names) + 1:]
    me = lax.axis_index("gx")
    core = lax.axis_index("gy")
    other = 1 - core
    rows_x = recv_1.shape[4]
    quarter = n * rows_x
    part_cells = cells // HALVES
    here = dict(field=signal, spectral=weights, mixing=mixing, bias=bias, zf=zf, yf=yf, xf=xf, order=order,
                spread=spread, gather=gather, back=back, xb=xb, yb=yb, zb=zb, tile=tile, across=across)
    loads = {}
    for at, name in enumerate(("field", "zf", "yf", "xf", "order", "spread", "spectral", "gather", "back", "xb",
                               "yb", "mixing", "bias", "tile", "across", "zb")):
        source = hbm[name].at[core] if name in ("yf", "yb") else hbm[name]
        loads[name] = pltpu.make_async_copy(source, here[name], load_sem.at[at])
        loads[name].start()

    barrier = pltpu.get_barrier_semaphore()

    def greet(k, _):
        pl.semaphore_signal(barrier, inc=1, device_id={"gx": lax.rem(me + k, n)}, device_id_type=MESH)
        return 0

    lax.fori_loop(1, n, greet, 0)
    pl.semaphore_signal(barrier, inc=1, device_id={"gy": other}, device_id_type=MESH)

    def copy_to(send, recv, sems, peer, slot):
        return pltpu.make_async_remote_copy(
            src_ref=send.at[peer],
            dst_ref=recv.at[slot],
            send_sem=sems[0].at[peer],
            recv_sem=sems[1].at[slot],
            device_id={"gx": peer},
            device_id_type=MESH,
        )

    def exchange(send, recv, sems):
        def start(k, _):
            peer = lax.rem(me + k, n)
            copy_to(send, recv, sems, peer, me).start()
            return 0

        lax.fori_loop(1, n, start, 0)
        recv[me] = send[me]

    def arrive(send, recv, sems):
        def wait(k, _):
            peer = lax.rem(me + k, n)
            copy_to(send, recv, sems, peer, peer).wait()
            return 0

        lax.fori_loop(1, n, wait, 0)

    def outer(way, layer, j, h):
        sends, recvs = ((send_1, recv_1), (send_4, recv_4))[way]
        return (sends.at[layer, j, h], recvs.at[layer, j, h],
                (outer_send.at[way, layer, j, h], outer_recv.at[way, layer, j, h]))

    def inner(way, layer, j):
        sends, recvs = ((send_2, recv_2), (send_3, recv_3))[way]
        return (sends.at[layer, j], recvs.at[layer, j],
                (inner_send.at[way, layer, j], inner_recv.at[way, layer, j]))

    def pair_copy(way, layer, h, arriving=False):
        if way == 0:
            src, dst = send_y.at[layer, h, other], recv_y.at[layer, h]
        else:
            src, dst = both.at[layer, h, core], both.at[layer, h, other if arriving else core]
        return pltpu.make_async_remote_copy(
            src_ref=src,
            dst_ref=dst,
            send_sem=pair_send.at[way, layer, h],
            recv_sem=pair_recv.at[way, layer, h],
            device_id={"gy": other},
            device_id_type=MESH,
        )

    def z_forward(h):
        rows = pl.ds(h * part_cells, part_cells)

        def one(t, _):
            lanes = pl.ds(pl.multiple_of(t * 256, 256), 256)
            value = dot3((s_high[rows, :], s_low[rows, :]), (zf[0, :, lanes], zf[1, :, lanes]))
            per = WIDTH // 256
            to_rows = pl.ds(pl.multiple_of((t // per) * part_cells, part_cells), part_cells)
            to = pl.ds(pl.multiple_of((t % per) * 256, 256), 256)
            z_high[to_rows, to], z_low[to_rows, to] = split(value)
            return 0

        lax.fori_loop(0, 2 * WIDTH // 256, one, 0, unroll=UNROLL)

    def y_forward(layer, h):
        value = dot3((yf[0], yf[1]), (z_high[...], z_low[...]))
        send_y[layer, h] = value.reshape(2, quarter, WIDTH)
        pair_copy(0, layer, h).start()

    def x_send(layer, h):
        pair_copy(0, layer, h).wait()
        for j in range(CHUNKS):
            lanes = slice(j * CW, (j + 1) * CW)
            value = send_y[layer, h, core, :, lanes] + recv_y[layer, h, :, lanes]
            send_1[layer, j, h] = value.reshape(n, rows_x, CW)
            exchange(*outer(0, layer, j, h))

    def x_forward(layer, j):
        for h in range(HALVES):
            arrive(*outer(0, layer, j, h))
        value = dot3((xf[0], xf[1]), split(recv_1[layer, j].reshape(HALVES * quarter, CW)))
        send_2[layer, j] = value.reshape(send_2.shape[2:])
        exchange(*inner(0, layer, j))

    def mix(layer, j):
        arrive(*inner(0, layer, j))
        high, low = split(recv_2[layer, j].reshape(order.shape[1], CW))
        high = dot(order[...], high).astype(jnp.bfloat16)
        low = dot(order[...], low).astype(jnp.bfloat16)
        kept = order.shape[0]
        left = jnp.concatenate(
            [
                jnp.concatenate([high[:, b * 128:(b + 1) * 128], low[:, b * 128:(b + 1) * 128]], 1)
                for b in range(BLOCKS)
            ],
            0,
        )
        for k in range(8):
            modes = dot(left, spread[k])
            for b in range(BLOCKS):
                lanes = pl.ds(((j * BLOCKS + b) * 8 + k) * 256, 256)
                for p in range(pn):
                    at = b * kept + p * 32
                    real, imaginary = modes[at:at + 16], modes[at + 16:at + 32]
                    w_real = weights[layer, p, 0, :, lanes]
                    w_imaginary = weights[layer, p, 1, :, lanes]
                    for shift, term in (
                        (0, real * w_real - imaginary * w_imaginary),
                        (16, real * w_imaginary + imaginary * w_real),
                    ):
                        high, low = split(term[:, :128] + term[:, 128:])
                        product[at + shift:at + shift + 16, k * 256:k * 256 + 128] = high
                        product[at + shift:at + shift + 16, k * 256 + 128:k * 256 + 256] = low
        total = dot(product[...], gather[...])
        mixed = jnp.concatenate([total[b * kept:(b + 1) * kept, :] for b in range(BLOCKS)], 1)
        high, low = split(mixed)
        send_3[layer, j] = (dot(back[...], high) + dot(back[...], low)).reshape(send_3.shape[2:])
        exchange(*inner(1, layer, j))

    def x_backward(layer, j):
        arrive(*inner(1, layer, j))
        value = dot3((xb[0], xb[1]), split(recv_3[layer, j].reshape(order.shape[1], CW)))
        send_4[layer, j] = value.reshape(send_4.shape[2:])
        for h in range(HALVES):
            exchange(*outer(1, layer, j, h))

    def y_send(layer, h):
        for j in range(CHUNKS):
            arrive(*outer(1, layer, j, h))
            both[layer, h, core, :, j * CW:(j + 1) * CW] = recv_4[layer, j, h].reshape(quarter, CW)
        pair_copy(1, layer, h).start()

    def y_backward(layer, h):
        pair_copy(1, layer, h, arriving=True).wait()
        high, low = split(both[layer, h].reshape(2 * quarter, WIDTH))
        for part in range(2):
            at = slice(part * part_cells, (part + 1) * part_cells)
            lanes = slice(part * WIDTH, (part + 1) * WIDTH)
            b_high[:, lanes], b_low[:, lanes] = split(dot3((yb[0, at, :], yb[1, at, :]), (high, low)))

    def z_backward(layer, h):
        rows = pl.ds(h * part_cells, part_cells)
        local = (local_high[layer], local_low[layer])

        def one(t, _):
            lanes = pl.ds(pl.multiple_of(t * 256, 256), 256)
            value = dot3((b_high[...], b_low[...]), (zb[0, :, lanes], zb[1, :, lanes]))
            value += dot3((s_high[rows, lanes], s_low[rows, lanes]), local)
            value += wide_bias[layer]
            value = 0.5 * value * (1.0 + erf(value * math.sqrt(0.5)))
            signal[rows, lanes] = value
            s_high[rows, lanes], s_low[rows, lanes] = split(value)
            return 0

        lax.fori_loop(0, LANES // 256, one, 0, unroll=UNROLL)

    loads["field"].wait()

    def split_rows(i, _):
        at = pl.ds(pl.multiple_of(i * 64, 64), 64)
        s_high[at, :], s_low[at, :] = split(signal[at, :])
        return 0

    lax.fori_loop(0, cells // 64, split_rows, 0)
    loads["zf"].wait()
    z_forward(0)
    pl.semaphore_wait(barrier, n)
    loads["yf"].wait()
    y_forward(0, 0)
    z_forward(1)
    x_send(0, 0)
    y_forward(0, 1)
    for name in ("mixing", "bias", "tile", "across"):
        loads[name].wait()
    same = (lax.broadcasted_iota(jnp.int32, (256, 256), 0) // C
            == lax.broadcasted_iota(jnp.int32, (256, 256), 1) // C)
    for layer in range(LAYERS):
        for term, to in zip(split(mixing[layer]), (local_high, local_low)):
            wide = dot(dot(tile[...], term).astype(jnp.bfloat16), across[...])
            to[layer] = jnp.where(same, wide, 0.0).astype(jnp.bfloat16)
        high, rest = split(bias[layer:layer + 1, :])
        middle, low = split(bias[layer:layer + 1, :] - high.astype(jnp.float32))
        wide_bias[layer] = dot(high, across[...]) + (dot(middle, across[...]) + dot(low, across[...]))
    x_send(0, 1)
    for name in ("xf", "order", "spread", "spectral", "gather", "back", "xb", "yb", "zb"):
        loads[name].wait()

    def run_layer(layer, _):
        for stage in (x_forward, mix, x_backward):
            for j in range(CHUNKS):
                stage(layer, j)
        more = layer + 1 < LAYERS
        y_send(layer, 0)
        y_backward(layer, 0)
        z_backward(layer, 0)

        @pl.when(more)
        def _():
            z_forward(0)
            y_forward(layer + 1, 0)

        y_send(layer, 1)

        @pl.when(more)
        def _():
            x_send(layer + 1, 0)

        y_backward(layer, 1)
        z_backward(layer, 1)

        @pl.when(more)
        def _():
            z_forward(1)
            y_forward(layer + 1, 1)
            x_send(layer + 1, 1)

        return 0

    lax.fori_loop(0, LAYERS, run_layer, 0)
    store = pltpu.make_async_copy(signal, out_hbm, store_sem)
    store.start()
    store.wait()


def shards(field, spectral, mixing, bias):
    cells_x, cells_y = field.shape[:2]
    n, pair_size = lax.axis_size("gx"), lax.axis_size("gy")
    cells = cells_x * cells_y
    table = tables(n, pair_size, cells_x, cells_y)
    pn = spectral.shape[1]
    qs = spectral.shape[3]
    rows_x = cells_x // HALVES * (qs // n) * 2
    rows_p = table["xf"].shape[1] // n
    operands = [field.reshape(cells, LANES), spectral, mixing, bias] + [
        jnp.asarray(table[name])
        for name in ("zf", "yf", "xf", "order", "spread", "gather", "back", "xb", "yb", "zb", "tile", "across")
    ]
    f32, bf16 = jnp.float32, jnp.bfloat16
    scratch = []
    for at, operand in enumerate(operands):
        shape = operand.shape[1:] if at in (5, 12) else operand.shape
        scratch.append(pltpu.VMEM(shape, operand.dtype))
    quarter = n * rows_x
    kept = pn * 2 * qs
    part_cells = cells // HALVES
    scratch += [pltpu.VMEM((cells, LANES), bf16)] * 2
    scratch += [pltpu.VMEM((2 * part_cells, WIDTH), bf16)] * 2
    scratch += [pltpu.VMEM((part_cells, 2 * WIDTH), bf16)] * 2
    scratch += [
        pltpu.VMEM((BLOCKS * kept, 8 * 256), bf16),
        pltpu.VMEM((LAYERS, 256, 256), bf16),
        pltpu.VMEM((LAYERS, 256, 256), bf16),
        pltpu.VMEM((LAYERS, 1, 256), f32),
        pltpu.VMEM((LAYERS, HALVES, 2, quarter, WIDTH), f32),
        pltpu.VMEM((LAYERS, HALVES, quarter, WIDTH), f32),
    ]
    for shape in ((HALVES, n, rows_x), (n, rows_p), (n, rows_p), (HALVES, n, rows_x)):
        scratch += [pltpu.VMEM((LAYERS, CHUNKS) + shape + (CW,), f32)] * 2
    scratch += [
        pltpu.VMEM((LAYERS, HALVES, 2, quarter, WIDTH), f32),
        pltpu.SemaphoreType.DMA((len(operands),)),
        pltpu.SemaphoreType.DMA,
        pltpu.SemaphoreType.DMA((2, LAYERS, HALVES)),
        pltpu.SemaphoreType.DMA((2, LAYERS, HALVES)),
        pltpu.SemaphoreType.DMA((2, LAYERS, CHUNKS, HALVES, n)),
        pltpu.SemaphoreType.DMA((2, LAYERS, CHUNKS, HALVES, n)),
        pltpu.SemaphoreType.DMA((2, LAYERS, CHUNKS, n)),
        pltpu.SemaphoreType.DMA((2, LAYERS, CHUNKS, n)),
    ]
    result = pl.pallas_call(
        functools.partial(kernel, n, pn, cells),
        out_shape=jax.ShapeDtypeStruct((cells, LANES), f32),
        in_specs=[pl.BlockSpec(memory_space=pl.ANY)] * len(operands),
        out_specs=pl.BlockSpec(memory_space=pl.ANY),
        scratch_shapes=scratch,
        compiler_params=pltpu.CompilerParams(
            collective_id=0, has_side_effects=True, vmem_limit_bytes=60 * 1024 * 1024
        ),
    )(*operands)
    return result.reshape(cells_x, cells_y, LANES)


def solution(mesh):
    placed = (P(("groups", "gx"), "gy", None), P(None, "gx", None, "gy", None), P(), P())
    return jax.shard_map(
        shards,
        mesh=mesh,
        in_specs=placed,
        out_specs=P(("groups", "gx"), "gy", None),
        check_vma=False,
    )
```

```python
import functools
import math

import jax
import jax.numpy as jnp
import ml_dtypes
import numpy as np
from jax import lax
from jax.experimental import pallas as pl
from jax.experimental.pallas import tpu as pltpu
from jax.sharding import PartitionSpec as P

C = 16
MX = 32
MY = 32
MZ = 32
NZ = 64
LAYERS = 2
WIDTH = MZ * C
LANES = NZ * C
CHUNKS = 2
CW = WIDTH // CHUNKS
BLOCKS = CW // 128
UNROLL = 4
HALVES = 2
MESH = pl.DeviceIdType.MESH


def signed_modes(count):
    half = count // 2
    return np.concatenate([np.arange(half), np.arange(half) - half])


def waves(frequencies, positions, length):
    angle = 2.0 * math.pi * ((frequencies[:, None] * positions[None, :]) % length) / length
    return np.cos(angle), np.sin(angle)


def pair(matrix):
    high = matrix.astype(np.float32).astype(ml_dtypes.bfloat16)
    low = (matrix - high.astype(np.float64)).astype(np.float32).astype(ml_dtypes.bfloat16)
    return np.stack([high, low])


def complex_rows(cosine, sine, sign):
    return np.stack([np.stack([cosine, -sign * sine], -1), np.stack([sign * sine, cosine], -1)], -2)


@functools.lru_cache(None)
def tables(n, pair_size, cells_x, cells_y):
    span_x, span_y = cells_x * n, cells_y * pair_size
    qs = MY // pair_size
    group = n // 2
    qn, pn = qs // group, MX // n
    eye = np.eye
    part_x = cells_x // HALVES
    cosine, sine = waves(np.arange(MZ), np.arange(NZ), NZ)
    channels = eye(C)
    z_forward = np.einsum("pkz,cd->zcpkd", np.stack([cosine, -sine]), channels).reshape(LANES, 2 * WIDTH)
    scale = np.where(np.arange(MZ) == 0, 1.0, 2.0)[:, None] / (span_x * span_y * NZ)
    z_backward = np.einsum("pkz,cd->pkczd", np.stack([cosine * scale, -sine * scale]), channels).reshape(
        2 * WIDTH, LANES
    )
    y_forward, y_backward = [], []
    for g in range(pair_size):
        cosine, sine = waves(signed_modes(MY), g * cells_y + np.arange(cells_y), span_y)
        forward = complex_rows(cosine, sine, -1).reshape(pair_size, group, qn, cells_y, 2, 2)
        y_forward.append(
            pair(
                np.einsum("hdqyab,xw->hdxqabwy", forward, eye(part_x)).reshape(
                    pair_size * group * part_x * qn * 2, 2 * part_x * cells_y
                )
            )
        )
        backward = complex_rows(cosine, sine, 1).reshape(pair_size, group, qn, cells_y, 2, 2)
        y_backward.append(
            pair(
                np.einsum("hdqyab,xw->awyhdxqb", backward, eye(part_x)).reshape(
                    2 * part_x * cells_y, pair_size * group * part_x * qn * 2
                )
            )
        )
    cosine, sine = waves(signed_modes(MX), np.arange(span_x), span_x)
    rows = pn * qn * 2
    padded = max(8, rows)
    forward = complex_rows(cosine, sine, -1).reshape(n, pn, 2, group, HALVES, part_x, 2, 2)
    x_forward = np.einsum("dpgshxab,qr->gdpqahsxrb", forward, eye(qn)).reshape(2, n, rows, -1)
    x_forward = np.pad(x_forward, ((0, 0), (0, 0), (0, padded - rows), (0, 0))).reshape(2, n * padded, -1)
    backward = complex_rows(cosine, sine, 1).reshape(n, pn, 2, group, HALVES, part_x, 2, 2)
    x_backward = np.einsum("dpgshxab,qr->ghsxqadprb", backward, eye(qn)).reshape(2, HALVES * group * part_x * qn * 2, n, rows)
    x_backward = np.pad(x_backward, ((0, 0), (0, 0), (0, 0), (0, padded - rows))).reshape(2, -1, n * padded)
    order = np.zeros((pn, 2, group, qn, n, padded))
    for p in range(pn):
        for part in range(2):
            for s in range(n):
                for q in range(qn):
                    order[p, part, s % group, q, s, (p * qn + q) * 2 + part] = 1.0
    order = order.reshape(pn * 2 * qs, n * padded)
    spread = np.einsum("kl,cd,o->lckdo", eye(8), channels, np.ones(C)).reshape(128, 8, C * C)
    spread = np.concatenate([spread, spread]).transpose(1, 0, 2)
    gather = np.einsum("kl,c,op->kcolp", eye(8), np.ones(8), channels).reshape(8, 128, 128)
    gather = np.concatenate([gather, gather], 1).reshape(8 * 256, 128)
    tile = np.kron(np.ones((16, 1)), channels)
    cast = lambda a: np.ascontiguousarray(a).astype(ml_dtypes.bfloat16)
    return dict(
        zf=pair(z_forward),
        zb=pair(z_backward),
        yf=np.stack(y_forward),
        yb=np.stack(y_backward),
        xf=np.stack([pair(x_forward[g]) for g in range(2)]),
        xb=np.stack([pair(x_backward[g]) for g in range(2)]),
        order=cast(order),
        back=cast(order.T),
        spread=cast(spread),
        gather=cast(gather),
        tile=cast(tile),
        across=cast(tile.T),
    )


def split(value):
    high = value.astype(jnp.bfloat16)
    return high, (value - high.astype(jnp.float32)).astype(jnp.bfloat16)


def dot(left, right):
    return jnp.dot(left, right, preferred_element_type=jnp.float32)


def dot3(left, right):
    return dot(left[0], right[0]) + (dot(left[0], right[1]) + dot(left[1], right[0]))


def erf(x):
    x = jnp.clip(x, -4.0, 4.0)
    square = x * x
    top = jnp.float32(-2.72614225801306e-10)
    for c in (2.77068142495902e-08, -2.10102402082508e-06, -5.69250639462346e-05,
              -7.34990630326855e-04, -2.95459980854025e-03, -1.60960333262415e-02):
        top = top * square + c
    bottom = jnp.float32(-1.45660718464996e-05)
    for c in (-2.13374055278905e-04, -1.68282697438203e-03, -7.37332916720468e-03, -1.42647390514189e-02):
        bottom = bottom * square + c
    return x * top / bottom


def kernel(n, pn, cells, *refs):
    names = ("field", "spectral", "mixing", "bias", "zf", "yf", "xf", "order", "spread", "gather",
             "back", "xb", "yb", "zb", "tile", "across")
    hbm = dict(zip(names, refs))
    out_hbm = refs[len(names)]
    (signal, weights, mixing, bias, zf, yf, xf, order, spread, gather, back, xb, yb, zb, tile, across,
     s_high, s_low, z_high, z_low, b_high, b_low, product, local_high, local_low, wide_bias,
     send_y, recv_y, send_1, recv_1, send_2, recv_2, send_3, recv_3, send_4, recv_4, both,
     load_sem, store_sem, pair_send, pair_recv, outer_send, outer_recv, inner_send, inner_recv) = refs[len(names) + 1:]
    me = lax.axis_index("gx")
    core = lax.axis_index("gy")
    other = 1 - core
    rows_x = recv_1.shape[4]
    group = n // 2
    mine = lax.rem(me, group)
    base = me - mine
    quarter = group * rows_x
    part_cells = cells // HALVES
    here = dict(field=signal, spectral=weights, mixing=mixing, bias=bias, zf=zf, yf=yf, xf=xf, order=order,
                spread=spread, gather=gather, back=back, xb=xb, yb=yb, zb=zb, tile=tile, across=across)
    loads = {}
    for at, name in enumerate(("field", "zf", "yf", "xf", "order", "spread", "spectral", "gather", "back", "xb",
                               "yb", "mixing", "bias", "tile", "across", "zb")):
        source = hbm[name]
        if name in ("yf", "yb"):
            source = source.at[core]
        elif name in ("xf", "xb"):
            source = source.at[me // group]
        loads[name] = pltpu.make_async_copy(source, here[name], load_sem.at[at])
        loads[name].start()

    barrier = pltpu.get_barrier_semaphore()

    def greet(k, _):
        pl.semaphore_signal(barrier, inc=1, device_id={"gx": lax.rem(me + k, n)}, device_id_type=MESH)
        return 0

    lax.fori_loop(1, n, greet, 0)
    pl.semaphore_signal(barrier, inc=1, device_id={"gy": other}, device_id_type=MESH)

    def copy_to(send, recv, sems, first, peer, slot):
        return pltpu.make_async_remote_copy(
            src_ref=send.at[peer],
            dst_ref=recv.at[slot],
            send_sem=sems[0].at[peer],
            recv_sem=sems[1].at[slot],
            device_id={"gx": first + peer},
            device_id_type=MESH,
        )

    def exchange(send, recv, sems, first, own, size):
        def start(k, _):
            peer = lax.rem(own + k, size)
            copy_to(send, recv, sems, first, peer, own).start()
            return 0

        lax.fori_loop(1, size, start, 0)
        recv[own] = send[own]

    def arrive(send, recv, sems, first, own, size):
        def wait(k, _):
            peer = lax.rem(own + k, size)
            copy_to(send, recv, sems, first, peer, peer).wait()
            return 0

        lax.fori_loop(1, size, wait, 0)

    def outer(way, layer, j, h):
        sends, recvs = ((send_1, recv_1), (send_4, recv_4))[way]
        return (sends.at[layer, j, h], recvs.at[layer, j, h],
                (outer_send.at[way, layer, j, h], outer_recv.at[way, layer, j, h]), base, mine, group)

    def inner(way, layer, j):
        sends, recvs = ((send_2, recv_2), (send_3, recv_3))[way]
        return (sends.at[layer, j], recvs.at[layer, j],
                (inner_send.at[way, layer, j], inner_recv.at[way, layer, j]), 0, me, n)

    def pair_copy(way, layer, h, arriving=False):
        if way == 0:
            src, dst = send_y.at[layer, h, other], recv_y.at[layer, h]
        else:
            src, dst = both.at[layer, h, core], both.at[layer, h, other if arriving else core]
        return pltpu.make_async_remote_copy(
            src_ref=src,
            dst_ref=dst,
            send_sem=pair_send.at[way, layer, h],
            recv_sem=pair_recv.at[way, layer, h],
            device_id={"gy": other},
            device_id_type=MESH,
        )

    def z_forward(h):
        rows = pl.ds(h * part_cells, part_cells)

        def one(t, _):
            lanes = pl.ds(pl.multiple_of(t * 256, 256), 256)
            value = dot3((s_high[rows, :], s_low[rows, :]), (zf[0, :, lanes], zf[1, :, lanes]))
            per = WIDTH // 256
            to_rows = pl.ds(pl.multiple_of((t // per) * part_cells, part_cells), part_cells)
            to = pl.ds(pl.multiple_of((t % per) * 256, 256), 256)
            z_high[to_rows, to], z_low[to_rows, to] = split(value)
            return 0

        lax.fori_loop(0, 2 * WIDTH // 256, one, 0, unroll=UNROLL)

    def y_forward(layer, h):
        value = dot3((yf[0], yf[1]), (z_high[...], z_low[...]))
        send_y[layer, h] = value.reshape(2, quarter, WIDTH)
        pair_copy(0, layer, h).start()

    def x_send(layer, h):
        pair_copy(0, layer, h).wait()
        for j in range(CHUNKS):
            lanes = slice(j * CW, (j + 1) * CW)
            value = send_y[layer, h, core, :, lanes] + recv_y[layer, h, :, lanes]
            send_1[layer, j, h] = value.reshape(group, rows_x, CW)
            exchange(*outer(0, layer, j, h))

    def x_forward(layer, j):
        for h in range(HALVES):
            arrive(*outer(0, layer, j, h))
        value = dot3((xf[0], xf[1]), split(recv_1[layer, j].reshape(HALVES * quarter, CW)))
        send_2[layer, j] = value.reshape(send_2.shape[2:])
        exchange(*inner(0, layer, j))

    def mix(layer, j):
        arrive(*inner(0, layer, j))
        high, low = split(recv_2[layer, j].reshape(order.shape[1], CW))
        high, low = split(dot(order[...], high) + dot(order[...], low))
        kept = order.shape[0]
        left = jnp.concatenate(
            [
                jnp.concatenate([high[:, b * 128:(b + 1) * 128], low[:, b * 128:(b + 1) * 128]], 1)
                for b in range(BLOCKS)
            ],
            0,
        )
        for k in range(8):
            modes = dot(left, spread[k])
            for b in range(BLOCKS):
                lanes = pl.ds(((j * BLOCKS + b) * 8 + k) * 256, 256)
                for p in range(pn):
                    at = b * kept + p * 32
                    real, imaginary = modes[at:at + 16], modes[at + 16:at + 32]
                    w_real = weights[layer, p, 0, :, lanes]
                    w_imaginary = weights[layer, p, 1, :, lanes]
                    for shift, term in (
                        (0, real * w_real - imaginary * w_imaginary),
                        (16, real * w_imaginary + imaginary * w_real),
                    ):
                        high, low = split(term[:, :128] + term[:, 128:])
                        product[at + shift:at + shift + 16, k * 256:k * 256 + 128] = high
                        product[at + shift:at + shift + 16, k * 256 + 128:k * 256 + 256] = low
        total = dot(product[...], gather[...])
        mixed = jnp.concatenate([total[b * kept:(b + 1) * kept, :] for b in range(BLOCKS)], 1)
        high, low = split(mixed)
        send_3[layer, j] = (dot(back[...], high) + dot(back[...], low)).reshape(send_3.shape[2:])
        exchange(*inner(1, layer, j))

    def x_backward(layer, j):
        arrive(*inner(1, layer, j))
        value = dot3((xb[0], xb[1]), split(recv_3[layer, j].reshape(order.shape[1], CW)))
        send_4[layer, j] = value.reshape(send_4.shape[2:])
        for h in range(HALVES):
            exchange(*outer(1, layer, j, h))

    def y_send(layer, h):
        for j in range(CHUNKS):
            arrive(*outer(1, layer, j, h))
            both[layer, h, core, :, j * CW:(j + 1) * CW] = recv_4[layer, j, h].reshape(quarter, CW)
        pair_copy(1, layer, h).start()

    def y_backward(layer, h):
        pair_copy(1, layer, h, arriving=True).wait()
        high, low = split(both[layer, h].reshape(2 * quarter, WIDTH))
        for part in range(2):
            at = slice(part * part_cells, (part + 1) * part_cells)
            lanes = slice(part * WIDTH, (part + 1) * WIDTH)
            b_high[:, lanes], b_low[:, lanes] = split(dot3((yb[0, at, :], yb[1, at, :]), (high, low)))

    def z_backward(layer, h):
        rows = pl.ds(h * part_cells, part_cells)
        local = (local_high[layer], local_low[layer])

        def one(t, _):
            lanes = pl.ds(pl.multiple_of(t * 256, 256), 256)
            value = dot3((b_high[...], b_low[...]), (zb[0, :, lanes], zb[1, :, lanes]))
            value += dot3((s_high[rows, lanes], s_low[rows, lanes]), local)
            value += wide_bias[layer]
            value = 0.5 * value * (1.0 + erf(value * math.sqrt(0.5)))
            signal[rows, lanes] = value
            s_high[rows, lanes], s_low[rows, lanes] = split(value)
            return 0

        lax.fori_loop(0, LANES // 256, one, 0, unroll=UNROLL)

    loads["field"].wait()

    def split_rows(i, _):
        at = pl.ds(pl.multiple_of(i * 64, 64), 64)
        s_high[at, :], s_low[at, :] = split(signal[at, :])
        return 0

    lax.fori_loop(0, cells // 64, split_rows, 0)
    loads["zf"].wait()
    z_forward(0)
    pl.semaphore_wait(barrier, n)
    loads["yf"].wait()
    y_forward(0, 0)
    z_forward(1)
    x_send(0, 0)
    y_forward(0, 1)
    for name in ("mixing", "bias", "tile", "across"):
        loads[name].wait()
    same = (lax.broadcasted_iota(jnp.int32, (256, 256), 0) // C
            == lax.broadcasted_iota(jnp.int32, (256, 256), 1) // C)
    for layer in range(LAYERS):
        for term, to in zip(split(mixing[layer]), (local_high, local_low)):
            wide = dot(dot(tile[...], term).astype(jnp.bfloat16), across[...])
            to[layer] = jnp.where(same, wide, 0.0).astype(jnp.bfloat16)
        high, rest = split(bias[layer:layer + 1, :])
        middle, low = split(bias[layer:layer + 1, :] - high.astype(jnp.float32))
        wide_bias[layer] = dot(high, across[...]) + (dot(middle, across[...]) + dot(low, across[...]))
    x_send(0, 1)
    for name in ("xf", "order", "spread", "spectral", "gather", "back", "xb", "yb", "zb"):
        loads[name].wait()

    def run_layer(layer, _):
        for stage in (x_forward, mix, x_backward):
            for j in range(CHUNKS):
                stage(layer, j)
        more = layer + 1 < LAYERS
        y_send(layer, 0)
        y_backward(layer, 0)
        z_backward(layer, 0)

        @pl.when(more)
        def _():
            z_forward(0)
            y_forward(layer + 1, 0)

        y_send(layer, 1)

        @pl.when(more)
        def _():
            x_send(layer + 1, 0)

        y_backward(layer, 1)
        z_backward(layer, 1)

        @pl.when(more)
        def _():
            z_forward(1)
            y_forward(layer + 1, 1)
            x_send(layer + 1, 1)

        return 0

    lax.fori_loop(0, LAYERS, run_layer, 0)
    store = pltpu.make_async_copy(signal, out_hbm, store_sem)
    store.start()
    store.wait()


def shards(field, spectral, mixing, bias):
    cells_x, cells_y = field.shape[:2]
    n, pair_size = lax.axis_size("gx"), lax.axis_size("gy")
    cells = cells_x * cells_y
    table = tables(n, pair_size, cells_x, cells_y)
    pn = spectral.shape[1]
    qs = spectral.shape[3]
    group = n // 2
    rows_x = cells_x // HALVES * (qs // group) * 2
    rows_p = table["xf"].shape[2] // n
    operands = [field.reshape(cells, LANES), spectral, mixing, bias] + [
        jnp.asarray(table[name])
        for name in ("zf", "yf", "xf", "order", "spread", "gather", "back", "xb", "yb", "zb", "tile", "across")
    ]
    f32, bf16 = jnp.float32, jnp.bfloat16
    scratch = []
    for at, operand in enumerate(operands):
        shape = operand.shape[1:] if at in (5, 6, 11, 12) else operand.shape
        scratch.append(pltpu.VMEM(shape, operand.dtype))
    quarter = group * rows_x
    kept = pn * 2 * qs
    part_cells = cells // HALVES
    scratch += [pltpu.VMEM((cells, LANES), bf16)] * 2
    scratch += [pltpu.VMEM((2 * part_cells, WIDTH), bf16)] * 2
    scratch += [pltpu.VMEM((part_cells, 2 * WIDTH), bf16)] * 2
    scratch += [
        pltpu.VMEM((BLOCKS * kept, 8 * 256), bf16),
        pltpu.VMEM((LAYERS, 256, 256), bf16),
        pltpu.VMEM((LAYERS, 256, 256), bf16),
        pltpu.VMEM((LAYERS, 1, 256), f32),
        pltpu.VMEM((LAYERS, HALVES, 2, quarter, WIDTH), f32),
        pltpu.VMEM((LAYERS, HALVES, quarter, WIDTH), f32),
    ]
    for shape in ((HALVES, group, rows_x), (n, rows_p), (n, rows_p), (HALVES, group, rows_x)):
        scratch += [pltpu.VMEM((LAYERS, CHUNKS) + shape + (CW,), f32)] * 2
    scratch += [
        pltpu.VMEM((LAYERS, HALVES, 2, quarter, WIDTH), f32),
        pltpu.SemaphoreType.DMA((len(operands),)),
        pltpu.SemaphoreType.DMA,
        pltpu.SemaphoreType.DMA((2, LAYERS, HALVES)),
        pltpu.SemaphoreType.DMA((2, LAYERS, HALVES)),
        pltpu.SemaphoreType.DMA((2, LAYERS, CHUNKS, HALVES, group)),
        pltpu.SemaphoreType.DMA((2, LAYERS, CHUNKS, HALVES, group)),
        pltpu.SemaphoreType.DMA((2, LAYERS, CHUNKS, n)),
        pltpu.SemaphoreType.DMA((2, LAYERS, CHUNKS, n)),
    ]
    result = pl.pallas_call(
        functools.partial(kernel, n, pn, cells),
        out_shape=jax.ShapeDtypeStruct((cells, LANES), f32),
        in_specs=[pl.BlockSpec(memory_space=pl.ANY)] * len(operands),
        out_specs=pl.BlockSpec(memory_space=pl.ANY),
        scratch_shapes=scratch,
        compiler_params=pltpu.CompilerParams(
            collective_id=0, has_side_effects=True, vmem_limit_bytes=60 * 1024 * 1024
        ),
    )(*operands)
    return result.reshape(cells_x, cells_y, LANES)


def solution(mesh):
    placed = (P(("groups", "gx"), "gy", None), P(None, "gx", None, "gy", None), P(), P())
    return jax.shard_map(
        shards,
        mesh=mesh,
        in_specs=placed,
        out_specs=P(("groups", "gx"), "gy", None),
        check_vma=False,
    )
```
